256 devices in a mesh: trainer: 64 (over z, x, core), mp: 4 (over y).
Axes of the slice: x: 4, y: 4, z: 8, core: 2. Of those that a mesh axis runs over, the one named last changes fastest.
Arguments:
- history: bfloat16 [3, 131072, 1024], P(None, 'trainer', 'mp'), may hold values from -6 to 6
- send_rows: int32 [64, 64, 48], P('trainer'), may hold values from 0 to 2047
- batch_ids: int32 [64, 1024], P('trainer'), may hold values from 0 to 2047, as said below
- block_cols: int32 [512, 12], P('trainer'), may hold values from 0 to 31, as said below
- block_count: int32 [512], P('trainer'), may hold values from 1 to 12, as said below
- adjacency: bfloat16 [512, 12, 128, 128], P('trainer'), may hold values from -0.15625 to 0.15625
- weights: bfloat16 [3, 1024, 1024], P(None, None, 'mp'), may hold values from -0.1875 to 0.1875
- cotangent: bfloat16 [65536, 1024], P('trainer', 'mp'), may hold values from -0.0234375 to 0.0234375
Outputs:
- fresh_history: bfloat16 [2, 131072, 1024], P(None, 'trainer', 'mp')
- final_output: bfloat16 [65536, 1024], P('trainer', 'mp')
- weight_grad: float32 [1024, 1024], P('trainer', 'mp')
The draws below stay inside these ranges and needn't reach their ends.
Inputs may be any that keep to these rules, and one draw needn't show every extreme that they name: `send_rows`: rows of the sending owner's own history. `batch_ids`: the 1024 entries of one trainer are distinct; at most half of a trainer's history rows are in its batch. `block_cols`: the 12 slots of one row block name distinct column blocks; blocks below 8 are batch rows, the rest halo rows. `block_count`: slots from the count on are ignored; in every draw some trainers have all row blocks at 12.
All inputs are finite; a program needn't handle non-finite values.
Results may differ from the reference program's by a relative error of at most 0.0054.
Values may be sent and summed in bfloat16 or wider, within the bound.
No kernel may reach another device: no remote copies, remote signals or barrier semaphores. Data moves between devices by JAX's collectives and lax.ppermute only.
A program may use at most 64 MiB of HBM per device.

```python
import math
import jax
import jax.numpy as jnp
from jax import lax

D = 1024
LAYERS = 3
BLK = 128
K_MAX = 12
B_DEV = 1024
HIST_DEV = 2048
H = 48
RB = 8
CB = 32
NODES_H = 131072
NODES_B = 65536
N_TRAINER = 64


def draw_batch_ids(key, part):
    key = jax.random.fold_in(key, 11)
    subkeys = jax.random.split(key, N_TRAINER)
    return jax.vmap(lambda single: jax.random.permutation(single, HIST_DEV)[:B_DEV])(subkeys).astype(jnp.int32)


def draw_block_cols(key, part):
    key = jax.random.fold_in(key, 12)
    subkeys = jax.random.split(key, N_TRAINER * RB)
    return jax.vmap(lambda single: jax.random.permutation(single, CB)[:K_MAX])(subkeys).astype(jnp.int32)


def draw_block_count(key, part):
    key = jax.random.fold_in(key, 13)
    first_key, second_key, third_key = jax.random.split(key, 3)
    base_counts = jax.random.randint(first_key, (N_TRAINER * RB,), max(1, K_MAX // 4), K_MAX + 1)
    heavy = jax.random.randint(second_key, (N_TRAINER,), 0, 4) == 0
    forced = jax.random.randint(third_key, (), 0, N_TRAINER)
    heavy = heavy | (jnp.arange(N_TRAINER) == forced)
    return jnp.where(jnp.repeat(heavy, RB), K_MAX, base_counts).astype(jnp.int32)


def with_ends(drawn, own_key, least, high):
    shape = drawn.shape
    index_at = [jax.random.randint(jax.random.fold_in(own_key, axis), (), 0, shape[axis]) for axis in range(len(shape))]
    drawn = drawn.at[tuple(index_at)].set(least)
    longest = shape.index(max(shape))
    index_at[longest] = (index_at[longest] + 1) % shape[longest]
    return drawn.at[tuple(index_at)].set(high)


def steps_of(own_key, extent, cuts, low, top_value):
    def one(axis_at, blocks):
        heights = jax.random.uniform(jax.random.fold_in(jax.random.fold_in(own_key, 6), axis_at), (blocks,), jnp.float32, low / len(cuts), top_value / len(cuts))
        return jnp.repeat(jnp.exp(heights), extent[axis_at] // blocks).reshape((-1,) + (1,) * (len(extent) - axis_at - 1))

    gain = one(*cuts[0])
    for cut in cuts[1:]:
        gain = gain * one(*cut)
    return gain


def gaussian(own_key, extent, width, reach, cuts=(), kind=jnp.bfloat16):
    result = jax.random.normal(own_key, extent, jnp.float32) * width
    if len(cuts) > 0:
        result = steps_of(own_key, extent, cuts, -0.22, 0.18) * result
    return jnp.clip(result, min=-reach, max=reach).astype(kind)


def setup_inputs(seed: int = 0) -> dict:
    streams_of = jax.random.split(jax.random.key(seed), 9)
    return {
        "history": gaussian(streams_of[0], (LAYERS, NODES_H, D), 1.0, 6.0, ((1, 64), (2, 4))),
        "send_rows": with_ends(jax.random.randint(streams_of[1], (N_TRAINER, N_TRAINER, H), 0, HIST_DEV), jax.random.fold_in(streams_of[1], 1), 0, HIST_DEV - 1).astype(jnp.int32),
        "batch_ids": draw_batch_ids(jax.random.fold_in(streams_of[8], 71), 0),
        "block_cols": draw_block_cols(jax.random.fold_in(streams_of[8], 71), 0),
        "block_count": draw_block_count(jax.random.fold_in(streams_of[8], 71), 0),
        "adjacency": gaussian(streams_of[5], (N_TRAINER * RB, K_MAX, BLK, BLK), (K_MAX * BLK) ** -0.5, 0.15625, ((0, 64),)),
        "weights": gaussian(streams_of[6], (LAYERS, D, D), D ** -0.5, 0.1875, ((2, 4),)),
        "cotangent": gaussian(streams_of[7], (NODES_B, D), NODES_B ** -0.5, 0.0234375, ((0, 64), (1, 4))),
    }


mixing = 0.1
strength = 0.5


def layer_share(layer_index):
    return math.log(strength / (layer_index + 1) + 1.0)


def aggregate_blocks(stacked, column_ids, counts, blocks_here):
    feature_width = stacked.shape[1]
    blocks = stacked.reshape(-1, BLK, feature_width)
    picked = blocks[column_ids]
    active = jnp.arange(column_ids.shape[1], dtype=jnp.int32)[None, :] < counts[:, None]
    masked = jnp.where(active[:, :, None, None], blocks_here, jnp.zeros_like(blocks_here))
    summed = jnp.einsum("rkij,rkjd->rid", masked.astype(jnp.float32), picked.astype(jnp.float32))
    return summed.reshape(-1, feature_width)


def reference(history, send_rows, batch_ids, block_cols, block_count, adjacency, weights, cotangent):
    owner_base = jnp.arange(N_TRAINER, dtype=jnp.int32)[:, None] * HIST_DEV

    def per_trainer(grad_total, trainer):
        flat_rows = (send_rows[:, trainer, :] + owner_base).reshape(-1)
        local_ids = batch_ids[trainer] + trainer * HIST_DEV
        column_ids = lax.dynamic_slice_in_dim(block_cols, trainer * RB, RB, 0)
        counts = lax.dynamic_slice_in_dim(block_count, trainer * RB, RB, 0)
        blocks_here = lax.dynamic_slice_in_dim(adjacency, trainer * RB, RB, 0)
        cotangent_rows = lax.dynamic_slice_in_dim(cotangent, trainer * B_DEV, B_DEV, 0)
        start_rows = history[0][local_ids]
        current = start_rows
        fresh_rows = []
        for layer_index in range(LAYERS):
            halo_rows = history[layer_index][flat_rows]
            stacked = jnp.concatenate([current, halo_rows], 0)
            aggregate = aggregate_blocks(stacked, column_ids, counts, blocks_here)
            support = ((1.0 - mixing) * aggregate + mixing * start_rows.astype(jnp.float32)).astype(jnp.bfloat16)
            share = layer_share(layer_index)
            mixed = (1.0 - share) * support.astype(jnp.float32) + share * jnp.dot(support, weights[layer_index], preferred_element_type=jnp.float32)
            if layer_index + 1 < LAYERS:
                current = jax.nn.relu(mixed).astype(jnp.bfloat16)
                fresh_rows.append(current)
        grad_total = grad_total + lax.dot_general(support, cotangent_rows, (((0,), (0,)), ((), ())), preferred_element_type=jnp.float32)
        return grad_total, (fresh_rows[0], fresh_rows[1], mixed.astype(jnp.bfloat16))

    grad_total, outputs = lax.scan(per_trainer, jnp.zeros((D, D), jnp.float32), jnp.arange(N_TRAINER, dtype=jnp.int32))
    all_ids = (batch_ids + owner_base).reshape(-1)
    fresh_history = jnp.stack([
        history[1].at[all_ids].set(outputs[0].reshape(-1, D)),
        history[2].at[all_ids].set(outputs[1].reshape(-1, D)),
    ])
    final_output = outputs[2].reshape(-1, D)
    weight_grad = grad_total * layer_share(LAYERS - 1)
    return fresh_history, final_output, weight_grad
```

```python
import functools
import math

import jax
import jax.numpy as jnp
from jax import lax
from jax.experimental import pallas as pl
from jax.experimental.pallas import tpu as pltpu
from jax.sharding import Mesh
from jax.sharding import PartitionSpec as P

LAYERS = 3
BLK = 128
FEAT = 256
BATCH = 1024
HALO = 3072
HIST = 2048
ROWS = 512
SLOTS = 12
RB = 8
TRAINER = ("z", "x", "core")

mixing = 0.1
strength = 0.5
bf16 = jnp.bfloat16
f32 = jnp.float32

VMEM = pl.BlockSpec(memory_space=pltpu.VMEM)
SMEM = pl.BlockSpec(memory_space=pltpu.SMEM)


def layer_share(layer_index):
    return math.log(strength / (layer_index + 1) + 1.0)


def params(mib):
    return pltpu.CompilerParams(vmem_limit_bytes=mib * 2**20)


def cost(flops, read):
    return pl.CostEstimate(flops=flops, bytes_accessed=read, transcendentals=0)


def one_hot_of(ids):
    at = lax.broadcasted_iota(jnp.int32, (BLK, HIST), 1)
    parts = [(at == ids[:, b : b + 1]).astype(f32).astype(bf16) for b in range(ids.shape[1])]
    return jnp.concatenate(parts, 0)


def pick(chosen, rows):
    return jnp.dot(chosen, rows, preferred_element_type=f32).astype(bf16)


def gather_first_kernel(ids_ref, history_ref, out_ref):
    out_ref[...] = pick(one_hot_of(ids_ref[0]), history_ref[0])


def gather_first(ids, history):
    steps = HALO // ROWS
    return pl.pallas_call(
        gather_first_kernel,
        grid=(steps,),
        in_specs=[
            pl.BlockSpec((1, BLK, ROWS // BLK), lambda i: (i, 0, 0)),
            pl.BlockSpec((1, HIST, FEAT), lambda i: (0, 0, 0)),
        ],
        out_specs=pl.BlockSpec((ROWS, FEAT), lambda i: (i, 0)),
        out_shape=jax.ShapeDtypeStruct((HALO, FEAT), bf16),
        compiler_params=params(32),
        cost_estimate=cost(2 * HALO * HIST * FEAT, 3 << 20),
        name="gather_first",
    )(ids, history)


def gather_rest_kernel(ids_ref, history_ref, one_ref, two_ref, start_ref):
    step = pl.program_id(0)
    chosen = one_hot_of(ids_ref[0])

    @pl.when(step >= 2)
    def _():
        one_ref[...] = pick(chosen, history_ref[1])
        two_ref[...] = pick(chosen, history_ref[2])

    @pl.when(step < 2)
    def _():
        start_ref[...] = pick(chosen, history_ref[0])


def gather_rest(ids, history):
    steps = (HALO + BATCH) // ROWS
    late = lambda i: (jnp.maximum(i - 2, 0), 0)
    return pl.pallas_call(
        gather_rest_kernel,
        grid=(steps,),
        in_specs=[
            pl.BlockSpec((1, BLK, ROWS // BLK), lambda i: (i, 0, 0)),
            pl.BlockSpec((LAYERS, HIST, FEAT), lambda i: (0, 0, 0)),
        ],
        out_specs=[
            pl.BlockSpec((ROWS, FEAT), late),
            pl.BlockSpec((ROWS, FEAT), late),
            pl.BlockSpec((ROWS, FEAT), lambda i: (jnp.minimum(i, 1), 0)),
        ],
        out_shape=[
            jax.ShapeDtypeStruct((HALO, FEAT), bf16),
            jax.ShapeDtypeStruct((HALO, FEAT), bf16),
            jax.ShapeDtypeStruct((BATCH, FEAT), bf16),
        ],
        compiler_params=params(32),
        cost_estimate=cost(2 * (2 * HALO + BATCH) * HIST * FEAT, 6 << 20),
        name="gather_rest",
    )(ids, history)


def aggregate_kernel(cols_ref, count_ref, rows_ref, halo_ref, start_ref, adj_ref, out_ref, x_ref, picked_ref):
    x_ref[:RB] = rows_ref[...].reshape(RB, BLK, FEAT)
    x_ref[RB:] = halo_ref[...].reshape(HALO // BLK, BLK, FEAT)

    @pl.loop(0, RB)
    def _(r):
        count = count_ref[r]
        parts = []
        for k in range(SLOTS):
            picked_ref[k * BLK : (k + 1) * BLK, :] = x_ref[cols_ref[r, k]]
            block = adj_ref[r, k]
            parts.append(jnp.where(k < count, block, jnp.zeros_like(block)))
        total = jnp.dot(jnp.concatenate(parts, 1), picked_ref[...], preferred_element_type=f32)
        at = pl.ds(pl.multiple_of(r * BLK, BLK), BLK)
        start = start_ref[at, :].astype(f32)
        out_ref[at, :] = ((1.0 - mixing) * total + mixing * start).astype(bf16)


def aggregate(cols, count, rows, halo, start, adjacency):
    return pl.pallas_call(
        aggregate_kernel,
        in_specs=[SMEM, SMEM, VMEM, VMEM, VMEM, VMEM],
        out_specs=VMEM,
        out_shape=jax.ShapeDtypeStruct((BATCH, FEAT), bf16),
        scratch_shapes=[
            pltpu.VMEM((RB + HALO // BLK, BLK, FEAT), bf16),
            pltpu.VMEM((SLOTS * BLK, FEAT), bf16),
        ],
        compiler_params=params(32),
        cost_estimate=cost(2 * BATCH * SLOTS * BLK * FEAT, 6 << 20),
        name="aggregate",
    )(cols, count, rows, halo, start, adjacency)


def shift(array, axis, size, by):
    return lax.ppermute(array, axis, [(i, (i + by) % size) for i in range(size)])


def ring_gather(rows):
    half = rows.shape[0] // 2
    up, low = rows[:half], rows[half:]
    left_up, right_low = shift(up, "y", 4, 1), shift(low, "y", 4, 3)
    left_low, right_up = shift(low, "y", 4, 1), shift(up, "y", 4, 3)
    far_up, far_low = shift(left_up, "y", 4, 1), shift(right_low, "y", 4, 3)
    return left_up, left_low, right_up, right_low, far_up, far_low


def mix_kernel(share, last, me_ref, own_ref, lu_ref, ll_ref, ru_ref, rl_ref, fu_ref, fl_ref, w_ref, out_ref):
    me = me_ref[0]

    def slab(by):
        at = lax.rem(me + by, 4) * FEAT
        return w_ref[0, pl.ds(pl.multiple_of(at, FEAT), FEAT), :]

    half = BATCH // 2
    for part, others in ((0, (lu_ref, ru_ref, fu_ref)), (1, (ll_ref, rl_ref, fl_ref))):
        at = slice(part * half, (part + 1) * half)
        own = own_ref[at, :]
        total = jnp.dot(own, slab(0), preferred_element_type=f32)
        for other, by in zip(others, (3, 1, 2)):
            total += jnp.dot(other[...], slab(by), preferred_element_type=f32)
        mixed = (1.0 - share) * own.astype(f32) + share * total
        out_ref[at, :] = (mixed if last else jnp.maximum(mixed, 0.0)).astype(bf16)


def mix(layer_index, me, support, others, weights):
    last = layer_index + 1 == LAYERS
    whole = lambda shape: pl.BlockSpec(shape, lambda i: (0,) * len(shape))
    return pl.pallas_call(
        functools.partial(mix_kernel, layer_share(layer_index), last),
        grid=(1,),
        in_specs=[SMEM, whole((BATCH, FEAT))]
        + [whole((BATCH // 2, FEAT))] * 6
        + [pl.BlockSpec((1, 4 * FEAT, FEAT), lambda i: (layer_index, 0, 0))],
        out_specs=whole((BATCH, FEAT)),
        out_shape=jax.ShapeDtypeStruct((BATCH, FEAT), bf16),
        compiler_params=params(32),
        cost_estimate=cost(2 * BATCH * 4 * FEAT * FEAT, 3 << 20),
        name="mix",
    )(me, support, *others, weights)


def write_kernel(ids_ref, history_ref, one_ref, two_ref, out_ref):
    base = pl.program_id(0) * ROWS
    at = lax.broadcasted_iota(jnp.int32, (ROWS, BATCH), 0) + base
    chosen = (at == ids_ref[...]).astype(f32)
    hit = jnp.max(chosen, axis=1, keepdims=True) > 0.0
    chosen = chosen.astype(bf16)
    for layer, rows in ((0, one_ref), (1, two_ref)):
        put = pick(chosen, rows[...])
        out_ref[layer] = jnp.where(hit, put, history_ref[layer + 1])


def write_rows(ids, history, one, two):
    return pl.pallas_call(
        write_kernel,
        grid=(HIST // ROWS,),
        in_specs=[
            pl.BlockSpec((1, BATCH), lambda i: (0, 0)),
            pl.BlockSpec((LAYERS, ROWS, FEAT), lambda i: (0, i, 0)),
            pl.BlockSpec((BATCH, FEAT), lambda i: (0, 0)),
            pl.BlockSpec((BATCH, FEAT), lambda i: (0, 0)),
        ],
        out_specs=pl.BlockSpec((2, ROWS, FEAT), lambda i: (0, i, 0)),
        out_shape=jax.ShapeDtypeStruct((2, HIST, FEAT), bf16),
        compiler_params=params(32),
        cost_estimate=cost(4 * BATCH * HIST * FEAT, 6 << 20),
        name="write_rows",
    )(ids, history, one, two)


def grad_kernel(core_ref, support_ref, cot_ref, keep_ref, send_ref, acc_ref):
    support = support_ref[...]
    for part in range(4):
        acc_ref[:, :, part * FEAT : (part + 1) * FEAT] = lax.dot_general(
            support, cot_ref[part], (((0,), (0,)), ((), ())), preferred_element_type=f32
        ).reshape(8, 32, FEAT)
    mine = pl.multiple_of(core_ref[0] * 16, 16)
    theirs = pl.multiple_of(16 - core_ref[0] * 16, 16)
    for group in range(8):
        keep_ref[group] = acc_ref[group, pl.ds(mine, 16), :]
        send_ref[group] = acc_ref[group, pl.ds(theirs, 16), :]


def grad_terms(core, support, cotangent):
    return pl.pallas_call(
        grad_kernel,
        in_specs=[SMEM, VMEM, VMEM],
        out_specs=[VMEM, VMEM],
        out_shape=[jax.ShapeDtypeStruct((8, 16, 4 * FEAT), f32)] * 2,
        scratch_shapes=[pltpu.VMEM((8, 32, 4 * FEAT), f32)],
        compiler_params=params(32),
        cost_estimate=cost(2 * BATCH * FEAT * 4 * FEAT, 4 << 20),
        name="grad_terms",
    )(core, support, cotangent)


def reduce_grad(keep, send):
    total = keep + shift(send, "core", 2, 1)
    total = total.reshape(2, 4, 16, 4, FEAT).transpose(1, 3, 0, 2, 4).reshape(16, 32, FEAT)
    total = lax.all_to_all(total, ("x", "y"), 0, 0, tiled=True)
    total = total.reshape(4, 8, 16, FEAT).sum(0)
    total = lax.all_to_all(total, "z", 0, 0, tiled=True)
    return total.sum(0) * layer_share(LAYERS - 1)


def body(history, send_rows, batch_ids, block_cols, block_count, adjacency, weights, cotangent):
    me = lax.axis_index("y").astype(jnp.int32).reshape(1)
    core = lax.axis_index("core").astype(jnp.int32).reshape(1)
    by_step = lambda ids: ids.reshape(-1, ROWS // BLK, BLK).transpose(0, 2, 1)
    send_ids = by_step(send_rows)
    batch = by_step(batch_ids)

    def exchange(rows):
        rows = rows.reshape(64, HALO // 64, FEAT)
        return lax.all_to_all(rows, TRAINER, 0, 0, tiled=True).reshape(HALO, FEAT)

    halo_0 = exchange(gather_first(send_ids, history))
    send_1, send_2, start = gather_rest(jnp.concatenate([batch, send_ids], 0), history)
    halo_1 = exchange(send_1)
    halo_2 = exchange(send_2)
    cot_all = lax.all_gather(cotangent, "y", axis=0, tiled=False)

    support = aggregate(block_cols, block_count, start, halo_0, start, adjacency)
    one = mix(0, me, support, ring_gather(support), weights)
    support = aggregate(block_cols, block_count, one, halo_1, start, adjacency)
    two = mix(1, me, support, ring_gather(support), weights)
    fresh = write_rows(batch_ids, history, one, two)
    support = aggregate(block_cols, block_count, two, halo_2, start, adjacency)
    grad = reduce_grad(*grad_terms(core, support, cot_all))
    final = mix(2, me, support, ring_gather(support), weights)
    return fresh, final, grad


def solution(mesh):
    fine = Mesh(mesh.devices.reshape(8, 4, 2, 4), ("z", "x", "core", "y"))
    return jax.shard_map(
        body,
        mesh=fine,
        in_specs=(
            P(None, TRAINER, "y"),
            P(TRAINER, None, None),
            P(TRAINER, None),
            P(TRAINER, None),
            P(TRAINER),
            P(TRAINER, None, None, None),
            P(None, None, "y"),
            P(TRAINER, "y"),
        ),
        out_specs=(P(None, TRAINER, "y"), P(TRAINER, "y"), P(TRAINER, "y")),
        check_vma=False,
    )
```

```python
import functools
import math

import jax
import jax.numpy as jnp
from jax import lax
from jax.experimental import pallas as pl
from jax.experimental.pallas import tpu as pltpu
from jax.sharding import Mesh
from jax.sharding import PartitionSpec as P

LAYERS = 3
BLK = 128
FEAT = 256
BATCH = 1024
HALF = 512
HALO = 3072
HIST = 2048
ROWS = 512
SLOTS = 12
RB = 8
HB = HALO // BLK
LATE = 10**11
TRAINER = ("z", "x", "core")

mixing = 0.1
strength = 0.5
bf16 = jnp.bfloat16
f32 = jnp.float32

VMEM = pl.BlockSpec(memory_space=pltpu.VMEM)
SMEM = pl.BlockSpec(memory_space=pltpu.SMEM)


def layer_share(layer_index):
    return math.log(strength / (layer_index + 1) + 1.0)


def call(kernel, name, flops, mib=24, **rest):
    return pl.pallas_call(
        kernel,
        name=name,
        compiler_params=pltpu.CompilerParams(vmem_limit_bytes=mib * 2**20),
        cost_estimate=pl.CostEstimate(flops=flops, bytes_accessed=4 << 20, transcendentals=0),
        **rest,
    )


def shape(*dims, dtype=bf16):
    return jax.ShapeDtypeStruct(dims, dtype)


def one_hot_of(ids):
    at = lax.broadcasted_iota(jnp.int32, (BLK, HIST), 1)
    parts = [(at == ids[:, b : b + 1]).astype(f32).astype(bf16) for b in range(ids.shape[1])]
    return jnp.concatenate(parts, 0)


def pick(chosen, rows):
    return jnp.dot(chosen, rows, preferred_element_type=f32).astype(bf16)


IDS = pl.BlockSpec((1, BLK, ROWS // BLK), lambda i: (i, 0, 0))


def send_first_kernel(ids_ref, rows_ref, out_ref):
    out_ref[...] = pick(one_hot_of(ids_ref[0]), rows_ref[...])


def send_first(ids, rows):
    return call(
        send_first_kernel,
        "send_first",
        2 * HALO * HIST * FEAT,
        grid=(HALO // ROWS,),
        in_specs=[IDS, pl.BlockSpec((HIST, FEAT), lambda i: (0, 0))],
        out_specs=pl.BlockSpec((ROWS, FEAT), lambda i: (i, 0)),
        out_shape=shape(HALO, FEAT),
    )(ids, rows)


def send_rest_kernel(ids_ref, zero_ref, one_ref, two_ref, send_one_ref, send_two_ref, start_ref):
    step = pl.program_id(0)
    chosen = one_hot_of(ids_ref[0])

    @pl.when(step >= 2)
    def _():
        send_one_ref[...] = pick(chosen, one_ref[0])
        send_two_ref[...] = pick(chosen, two_ref[0])

    @pl.when(step < 2)
    def _():
        start_ref[...] = pick(chosen, zero_ref[...])


def send_rest(ids, zero, history):
    late = lambda i: (jnp.maximum(i - 2, 0), 0)
    whole = lambda layer: pl.BlockSpec((1, HIST, FEAT), lambda i: (layer, 0, 0))
    return call(
        send_rest_kernel,
        "send_rest",
        2 * (2 * HALO + BATCH) * HIST * FEAT,
        grid=((HALO + BATCH) // ROWS,),
        in_specs=[IDS, pl.BlockSpec((HIST, FEAT), lambda i: (0, 0)), whole(1), whole(2)],
        out_specs=[
            pl.BlockSpec((ROWS, FEAT), late),
            pl.BlockSpec((ROWS, FEAT), late),
            pl.BlockSpec((ROWS, FEAT), lambda i: (jnp.minimum(i, 1), 0)),
        ],
        out_shape=[shape(HALO, FEAT), shape(HALO, FEAT), shape(BATCH, FEAT)],
    )(ids, zero, history, history)


def slab(w_ref, me, by):
    at = lax.rem(me + by, 4) * FEAT
    return w_ref[0, pl.ds(pl.multiple_of(at, FEAT), FEAT), :]


def mixed(share, me, w_ref, refs):
    own = refs[0][...]
    total = jnp.zeros(own.shape, f32)
    for ref, by in zip(refs, (0, 3, 1, 2)):
        total += jnp.dot(ref[...], slab(w_ref, me, by), preferred_element_type=f32)
    return (1.0 - share) * own.astype(f32) + share * total


def product(r, cols_ref, count_ref, adj_ref, x_ref):
    total = jnp.zeros((BLK, FEAT), f32)
    count = count_ref[r]
    for k in range(0, SLOTS, 2):
        left, right = [], []
        for slot in (k, k + 1):
            block = adj_ref[r, slot]
            left.append(jnp.where(slot < count, block, jnp.zeros_like(block)))
            right.append(x_ref[cols_ref[r, slot]])
        total += jnp.dot(jnp.concatenate(left, 1), jnp.concatenate(right, 0), preferred_element_type=f32)
    return total


def block(r):
    return pl.ds(r * BLK, BLK)


def put(up_ref, low_ref, r, value):
    ref = up_ref if r < RB // 2 else low_ref
    ref[block(r % (RB // 2)), :] = value


def supported(total, start_ref, r):
    return ((1.0 - mixing) * total + mixing * start_ref[block(r), :].astype(f32)).astype(bf16)


def layer_kernel(cols_ref, count_ref, up_ref, low_ref, halo_ref, start_ref, adj_ref, out_up_ref, out_low_ref, x_ref):
    x_ref[: RB // 2] = up_ref[...].reshape(RB // 2, BLK, FEAT)
    x_ref[RB // 2 : RB] = low_ref[...].reshape(RB // 2, BLK, FEAT)
    x_ref[RB:] = halo_ref[...].reshape(HB, BLK, FEAT)
    for r in range(RB):
        put(out_up_ref, out_low_ref, r, supported(product(r, cols_ref, count_ref, adj_ref, x_ref), start_ref, r))


def layer(cols, count, rows, halo, start, adjacency):
    return call(
        layer_kernel,
        "layer",
        2 * BATCH * SLOTS * BLK * FEAT,
        in_specs=[SMEM, SMEM] + [VMEM] * 5,
        out_specs=[VMEM, VMEM],
        out_shape=[shape(HALF, FEAT)] * 2,
        scratch_shapes=[pltpu.VMEM((RB + HB, BLK, FEAT), bf16)],
    )(cols, count, *rows, halo, start, adjacency)


def mix_kernel(share, me_ref, up_ref, low_ref, lu_ref, ll_ref, ru_ref, rl_ref, fu_ref, fl_ref, w_ref, out_up_ref, out_low_ref):
    me = me_ref[0]
    out_up_ref[...] = jnp.maximum(mixed(share, me, w_ref, (up_ref, lu_ref, ru_ref, fu_ref)), 0.0).astype(bf16)
    out_low_ref[...] = jnp.maximum(mixed(share, me, w_ref, (low_ref, ll_ref, rl_ref, fl_ref)), 0.0).astype(bf16)


def mix(index, me, rows, others, weights):
    half = pl.BlockSpec((HALF, FEAT), lambda i: (0, 0))
    return call(
        functools.partial(mix_kernel, layer_share(index)),
        "mix",
        2 * BATCH * 4 * FEAT * FEAT,
        grid=(1,),
        in_specs=[SMEM] + [half] * 8 + [pl.BlockSpec((1, 4 * FEAT, FEAT), lambda i: (index, 0, 0))],
        out_specs=[half, half],
        out_shape=[shape(HALF, FEAT)] * 2,
    )(me, *rows, *others, weights)


def mix_last_kernel(me_ref, up_ref, low_ref, lu_ref, ll_ref, ru_ref, rl_ref, fu_ref, fl_ref, w_ref, out_ref):
    me, share = me_ref[0], layer_share(2)
    out_ref[:HALF] = mixed(share, me, w_ref, (up_ref, lu_ref, ru_ref, fu_ref)).astype(bf16)
    out_ref[HALF:] = mixed(share, me, w_ref, (low_ref, ll_ref, rl_ref, fl_ref)).astype(bf16)


def mix_last(me, rows, others, weights):
    half = pl.BlockSpec((HALF, FEAT), lambda i: (0, 0))
    return call(
        mix_last_kernel,
        "mix_last",
        LATE,
        grid=(1,),
        in_specs=[SMEM] + [half] * 8 + [pl.BlockSpec((1, 4 * FEAT, FEAT), lambda i: (2, 0, 0))],
        out_specs=pl.BlockSpec((BATCH, FEAT), lambda i: (0, 0)),
        out_shape=shape(BATCH, FEAT),
    )(me, *rows, *others, weights)


def write_kernel(ids_ref, history_ref, *refs):
    base = pl.program_id(0) * ROWS
    at = lax.broadcasted_iota(jnp.int32, (ROWS, BATCH), 0) + base
    chosen = (at == ids_ref[...]).astype(f32)
    hit = jnp.max(chosen, axis=1, keepdims=True) > 0.0
    rows = jnp.concatenate([refs[0][...], refs[1][...]], 0)
    refs[-1][0] = jnp.where(hit, pick(chosen.astype(bf16), rows), history_ref[0])


def write_rows(layer, ids, history, rows, so_far=None):
    in_specs = [
        pl.BlockSpec((1, BATCH), lambda i: (0, 0)),
        pl.BlockSpec((1, ROWS, FEAT), lambda i: (layer + 1, i, 0)),
    ] + [pl.BlockSpec(part.shape, lambda i: (0, 0)) for part in rows]
    if so_far is not None:
        in_specs.append(pl.BlockSpec(memory_space=pl.ANY))
    return call(
        write_kernel,
        "write_rows",
        2 * BATCH * HIST * FEAT,
        grid=(HIST // ROWS,),
        in_specs=in_specs,
        out_specs=pl.BlockSpec((1, ROWS, FEAT), lambda i: (layer, i, 0)),
        out_shape=shape(2, HIST, FEAT),
        input_output_aliases={} if so_far is None else {len(in_specs) - 1: 0},
    )(ids, history, *rows, *(() if so_far is None else (so_far,)))


def grad_kernel(core_ref, me_ref, up_ref, low_ref, own_ref, left_ref, right_ref, far_ref, keep_ref, send_ref, acc_ref):
    support = jnp.concatenate([up_ref[...], low_ref[...]], 0)
    for by, ref in ((0, own_ref), (3, left_ref), (1, right_ref), (2, far_ref)):
        term = lax.dot_general(support, ref[...], (((0,), (0,)), ((), ())), preferred_element_type=f32)
        acc_ref[lax.rem(me_ref[0] + by, 4)] = term.reshape(8, 32, FEAT)
    mine = pl.multiple_of(core_ref[0] * 16, 16)
    theirs = pl.multiple_of(16 - core_ref[0] * 16, 16)
    for low in range(2):
        for x in range(4):
            group = low * 4 + x
            for y in range(4):
                keep_ref[x * 4 + y, low] = acc_ref[y, group, pl.ds(mine, 16), :]
                send_ref[x * 4 + y, low] = acc_ref[y, group, pl.ds(theirs, 16), :]


def grad_terms(core, me, support, own, parts):
    return call(
        grad_kernel,
        "grad_terms",
        2 * BATCH * FEAT * 4 * FEAT,
        in_specs=[SMEM, SMEM] + [VMEM] * 6,
        out_specs=[VMEM, VMEM],
        out_shape=[shape(16, 2, 16, FEAT, dtype=f32)] * 2,
        scratch_shapes=[pltpu.VMEM((4, 8, 32, FEAT), f32)],
    )(core, me, *support, own, *parts)


def shift(array, axis, size, by):
    return lax.ppermute(array, axis, [(i, (i + by) % size) for i in range(size)])


def ring_gather(up, low):
    left_up, right_low = shift(up, "y", 4, 1), shift(low, "y", 4, 3)
    left_low, right_up = shift(low, "y", 4, 1), shift(up, "y", 4, 3)
    far_up, far_low = shift(left_up, "y", 4, 1), shift(right_low, "y", 4, 3)
    return left_up, left_low, right_up, right_low, far_up, far_low


def halves(rows):
    return rows[: rows.shape[0] // 2], rows[rows.shape[0] // 2 :]


def after(value, *others):
    return lax.optimization_barrier((value, *others))[0]


def reduce_grad(keep, send):
    total = (keep + shift(send, "core", 2, 1)).astype(bf16).reshape(16, 32, FEAT)
    total = lax.all_to_all(total, ("x", "y"), 0, 0, tiled=True)
    total = total.reshape(4, 8, 16, FEAT).astype(f32).sum(0)
    across = lax.all_to_all(total, "z", 0, 0, tiled=True)
    return across.sum(0) * layer_share(LAYERS - 1)


def body(history, send_rows, batch_ids, block_cols, block_count, adjacency, weights, cotangent):
    me = lax.axis_index("y").astype(jnp.int32).reshape(1)
    core = lax.axis_index("core").astype(jnp.int32).reshape(1)
    by_step = lambda ids: ids.reshape(-1, ROWS // BLK, BLK).transpose(0, 2, 1)
    send_ids = by_step(send_rows)

    def exchange(rows):
        rows = rows.reshape(64, HALO // 64, FEAT)
        return lax.all_to_all(rows, TRAINER, 0, 0, tiled=True).reshape(HALO, FEAT)

    zero = history[0]
    sent = send_first(send_ids, zero)
    halo = exchange(sent)
    own_cot = after(cotangent, sent)
    others_cot = tuple(shift(own_cot, "y", 4, by) for by in (1, 3, 2))
    send_one, send_two, start = send_rest(jnp.concatenate([by_step(batch_ids), send_ids], 0), zero, history)
    halo_one = exchange(after(send_one, *others_cot))

    support = layer(block_cols, block_count, halves(start), halo, start, adjacency)
    one = mix(0, me, support, ring_gather(*support), weights)
    halo_two = exchange(after(send_two, *one))
    fresh = write_rows(0, batch_ids, history, one)
    support = layer(block_cols, block_count, one, halo_one, start, adjacency)
    two = mix(1, me, support, ring_gather(*support), weights)
    fresh = write_rows(1, batch_ids, history, two, fresh)
    support = layer(block_cols, block_count, after(tuple(two), fresh), halo_two, start, adjacency)
    others = ring_gather(*support)
    grad = reduce_grad(*grad_terms(core, me, support, cotangent, others_cot))
    final = mix_last(me, support, others, weights)
    return fresh, final, grad


def solution(mesh):
    fine = Mesh(mesh.devices.reshape(8, 4, 2, 4), ("z", "x", "core", "y"))
    return jax.shard_map(
        body,
        mesh=fine,
        in_specs=(
            P(None, TRAINER, "y"),
            P(TRAINER, None, None),
            P(TRAINER, None),
            P(TRAINER, None),
            P(TRAINER),
            P(TRAINER, None, None, None),
            P(None, None, "y"),
            P(TRAINER, "y"),
        ),
        out_specs=(P(None, TRAINER, "y"), P(TRAINER, "y"), P(TRAINER, "y")),
        check_vma=False,
    )
```

```python
import functools
import math

import jax
import jax.numpy as jnp
from jax import lax
from jax.experimental import pallas as pl
from jax.experimental.pallas import tpu as pltpu
from jax.sharding import Mesh
from jax.sharding import PartitionSpec as P

LAYERS = 3
BLK = 128
FEAT = 256
BATCH = 1024
HALF = 512
HALO = 3072
H = 48
CHIPS = 8
HIST = 2048
ROWS = 512
SLOTS = 12
RB = 8
HB = HALO // BLK
LATE = 10**11
TRAINER = ("z", "x", "core")

mixing = 0.1
strength = 0.5
bf16 = jnp.bfloat16
f32 = jnp.float32

VMEM = pl.BlockSpec(memory_space=pltpu.VMEM)
SMEM = pl.BlockSpec(memory_space=pltpu.SMEM)


def layer_share(layer_index):
    return math.log(strength / (layer_index + 1) + 1.0)


def call(kernel, name, flops, mib=12, **rest):
    return pl.pallas_call(
        kernel,
        name=name,
        compiler_params=pltpu.CompilerParams(vmem_limit_bytes=mib * 2**20),
        cost_estimate=pl.CostEstimate(flops=flops, bytes_accessed=4 << 20, transcendentals=0),
        **rest,
    )


def shape(*dims, dtype=bf16):
    return jax.ShapeDtypeStruct(dims, dtype)


def one_hot_of(ids):
    at = lax.broadcasted_iota(jnp.int32, (BLK, HIST), 1)
    parts = [(at == ids[:, b : b + 1]).astype(f32).astype(bf16) for b in range(ids.shape[1])]
    return jnp.concatenate(parts, 0)


def pick(chosen, rows):
    return jnp.dot(chosen, rows, preferred_element_type=f32).astype(bf16)


IDS = pl.BlockSpec((1, BLK, ROWS // BLK), lambda i: (i, 0, 0))


def send_first_kernel(ids_ref, rows_ref, out_ref):
    out_ref[...] = pick(one_hot_of(ids_ref[0]), rows_ref[...])


def send_first(ids, rows):
    return call(
        send_first_kernel,
        "send_first",
        2 * HALO * HIST * FEAT,
        grid=(HALO // ROWS,),
        in_specs=[IDS, pl.BlockSpec((HIST, FEAT), lambda i: (0, 0))],
        out_specs=pl.BlockSpec((ROWS, FEAT), lambda i: (i, 0)),
        out_shape=shape(HALO, FEAT),
    )(ids, rows)


def send_rest_kernel(core_ref, mine_ref, theirs_ref, own_one_ref, own_two_ref, other_ref, one_ref, two_ref):
    for core, ids_ref, one, two in (
        (core_ref[0], mine_ref, own_one_ref.at[0], own_two_ref.at[0]),
        (1 - core_ref[0], theirs_ref, other_ref.at[0], other_ref.at[1]),
    ):
        chosen = one_hot_of(ids_ref[0])
        one_ref[:, core] = pick(chosen, one[...]).reshape(CHIPS, H, FEAT)
        two_ref[:, core] = pick(chosen, two[...]).reshape(CHIPS, H, FEAT)


def send_rest(core, mine, theirs, history, other):
    ids = pl.BlockSpec((1, BLK, CHIPS * H // BLK), lambda i: (i, 0, 0))
    whole = lambda layer: pl.BlockSpec((1, HIST, FEAT), lambda i: (layer, 0, 0))
    rows = pl.BlockSpec((CHIPS, 2, H, FEAT), lambda i: (i, 0, 0, 0))
    return call(
        send_rest_kernel,
        "send_rest",
        4 * HALO * HIST * FEAT,
        mib=60,
        grid=(32 // CHIPS,),
        in_specs=[SMEM, ids, ids, whole(1), whole(2), pl.BlockSpec((2, HIST, FEAT), lambda i: (0, 0, 0))],
        out_specs=[rows, rows],
        out_shape=[shape(32, 2, H, FEAT)] * 2,
    )(core, mine, theirs, history, history, other)


def start_kernel(ids_ref, zero_ref, out_ref):
    out_ref[...] = pick(one_hot_of(ids_ref[0]), zero_ref[...])


def start_rows(ids, zero):
    return call(
        start_kernel,
        "start_rows",
        flops=2 * BATCH * HIST * FEAT,
        mib=60,
        grid=(BATCH // ROWS,),
        in_specs=[IDS, pl.BlockSpec((HIST, FEAT), lambda i: (0, 0))],
        out_specs=pl.BlockSpec((ROWS, FEAT), lambda i: (i, 0)),
        out_shape=shape(BATCH, FEAT),
    )(ids, zero)


def slab(w_ref, me, by):
    at = lax.rem(me + by, 4) * FEAT
    return w_ref[0, pl.ds(pl.multiple_of(at, FEAT), FEAT), :]


def mixed(share, me, w_ref, refs):
    own = refs[0][...]
    total = jnp.zeros(own.shape, f32)
    for ref, by in zip(refs, (0, 3, 1, 2)):
        total += jnp.dot(ref[...], slab(w_ref, me, by), preferred_element_type=f32)
    return (1.0 - share) * own.astype(f32) + share * total


def product(r, cols_ref, count_ref, adj_ref, x_ref):
    total = jnp.zeros((BLK, FEAT), f32)
    count = count_ref[r]
    for k in range(0, SLOTS, 2):
        left, right = [], []
        for slot in (k, k + 1):
            block = adj_ref[r, slot]
            left.append(jnp.where(slot < count, block, jnp.zeros_like(block)))
            right.append(x_ref[cols_ref[r, slot]])
        total += jnp.dot(jnp.concatenate(left, 1), jnp.concatenate(right, 0), preferred_element_type=f32)
    return total


def block(r):
    return pl.ds(r * BLK, BLK)


def put(up_ref, low_ref, r, value):
    ref = up_ref if r < RB // 2 else low_ref
    ref[block(r % (RB // 2)), :] = value


def supported(total, start_ref, r):
    return ((1.0 - mixing) * total + mixing * start_ref[block(r), :].astype(f32)).astype(bf16)


def layer_kernel(cols_ref, count_ref, up_ref, low_ref, halo_ref, start_ref, adj_ref, out_up_ref, out_low_ref, x_ref):
    x_ref[: RB // 2] = up_ref[...].reshape(RB // 2, BLK, FEAT)
    x_ref[RB // 2 : RB] = low_ref[...].reshape(RB // 2, BLK, FEAT)
    x_ref[RB:] = halo_ref[...].reshape(HB, BLK, FEAT)
    for r in range(RB):
        put(out_up_ref, out_low_ref, r, supported(product(r, cols_ref, count_ref, adj_ref, x_ref), start_ref, r))


def layer(cols, count, rows, halo, start, adjacency):
    return call(
        layer_kernel,
        "layer",
        2 * BATCH * SLOTS * BLK * FEAT,
        in_specs=[SMEM, SMEM] + [VMEM] * 5,
        out_specs=[VMEM, VMEM],
        out_shape=[shape(HALF, FEAT)] * 2,
        scratch_shapes=[pltpu.VMEM((RB + HB, BLK, FEAT), bf16)],
    )(cols, count, *rows, halo, start, adjacency)


def mix_kernel(share, me_ref, up_ref, low_ref, lu_ref, ll_ref, ru_ref, rl_ref, fu_ref, fl_ref, w_ref, out_up_ref, out_low_ref):
    me = me_ref[0]
    out_up_ref[...] = jnp.maximum(mixed(share, me, w_ref, (up_ref, lu_ref, ru_ref, fu_ref)), 0.0).astype(bf16)
    out_low_ref[...] = jnp.maximum(mixed(share, me, w_ref, (low_ref, ll_ref, rl_ref, fl_ref)), 0.0).astype(bf16)


def mix(index, me, rows, others, weights):
    half = pl.BlockSpec((HALF, FEAT), lambda i: (0, 0))
    return call(
        functools.partial(mix_kernel, layer_share(index)),
        "mix",
        2 * BATCH * 4 * FEAT * FEAT,
        grid=(1,),
        in_specs=[SMEM] + [half] * 8 + [pl.BlockSpec((1, 4 * FEAT, FEAT), lambda i: (index, 0, 0))],
        out_specs=[half, half],
        out_shape=[shape(HALF, FEAT)] * 2,
    )(me, *rows, *others, weights)


def mix_last_kernel(me_ref, up_ref, low_ref, lu_ref, ll_ref, ru_ref, rl_ref, fu_ref, fl_ref, w_ref, out_ref):
    me, share = me_ref[0], layer_share(2)
    out_ref[:HALF] = mixed(share, me, w_ref, (up_ref, lu_ref, ru_ref, fu_ref)).astype(bf16)
    out_ref[HALF:] = mixed(share, me, w_ref, (low_ref, ll_ref, rl_ref, fl_ref)).astype(bf16)


def mix_last(me, rows, others, weights):
    half = pl.BlockSpec((HALF, FEAT), lambda i: (0, 0))
    return call(
        mix_last_kernel,
        "mix_last",
        LATE,
        grid=(1,),
        in_specs=[SMEM] + [half] * 8 + [pl.BlockSpec((1, 4 * FEAT, FEAT), lambda i: (2, 0, 0))],
        out_specs=pl.BlockSpec((BATCH, FEAT), lambda i: (0, 0)),
        out_shape=shape(BATCH, FEAT),
    )(me, *rows, *others, weights)


def write_kernel(ids_ref, history_ref, *refs):
    base = pl.program_id(0) * ROWS
    at = lax.broadcasted_iota(jnp.int32, (ROWS, BATCH), 0) + base
    chosen = (at == ids_ref[...]).astype(f32)
    hit = jnp.max(chosen, axis=1, keepdims=True) > 0.0
    rows = jnp.concatenate([refs[0][...], refs[1][...]], 0)
    refs[-1][0] = jnp.where(hit, pick(chosen.astype(bf16), rows), history_ref[0])


def write_rows(layer, ids, history, rows, so_far=None):
    in_specs = [
        pl.BlockSpec((1, BATCH), lambda i: (0, 0)),
        pl.BlockSpec((1, ROWS, FEAT), lambda i: (layer + 1, i, 0)),
    ] + [pl.BlockSpec(part.shape, lambda i: (0, 0)) for part in rows]
    if so_far is not None:
        in_specs.append(pl.BlockSpec(memory_space=pl.ANY))
    return call(
        write_kernel,
        "write_rows",
        2 * BATCH * HIST * FEAT,
        grid=(HIST // ROWS,),
        in_specs=in_specs,
        out_specs=pl.BlockSpec((1, ROWS, FEAT), lambda i: (layer, i, 0)),
        out_shape=shape(2, HIST, FEAT),
        input_output_aliases={} if so_far is None else {len(in_specs) - 1: 0},
    )(ids, history, *rows, *(() if so_far is None else (so_far,)))


def grad_kernel(core_ref, me_ref, up_ref, low_ref, own_ref, left_ref, right_ref, far_ref, keep_ref, send_ref, acc_ref):
    support = jnp.concatenate([up_ref[...], low_ref[...]], 0)
    for by, ref in ((0, own_ref), (3, left_ref), (1, right_ref), (2, far_ref)):
        term = lax.dot_general(support, ref[...], (((0,), (0,)), ((), ())), preferred_element_type=f32)
        acc_ref[lax.rem(me_ref[0] + by, 4)] = term.reshape(8, 32, FEAT)
    mine = pl.multiple_of(core_ref[0] * 16, 16)
    theirs = pl.multiple_of(16 - core_ref[0] * 16, 16)
    for low in range(2):
        for x in range(4):
            group = low * 4 + x
            for y in range(4):
                keep_ref[x * 4 + y, low] = acc_ref[y, group, pl.ds(mine, 16), :]
                send_ref[x * 4 + y, low] = acc_ref[y, group, pl.ds(theirs, 16), :]


def grad_terms(core, me, support, own, parts):
    return call(
        grad_kernel,
        "grad_terms",
        2 * BATCH * FEAT * 4 * FEAT,
        in_specs=[SMEM, SMEM] + [VMEM] * 6,
        out_specs=[VMEM, VMEM],
        out_shape=[shape(16, 2, 16, FEAT, dtype=f32)] * 2,
        scratch_shapes=[pltpu.VMEM((4, 8, 32, FEAT), f32)],
    )(core, me, *support, own, *parts)


def shift(array, axis, size, by):
    return lax.ppermute(array, axis, [(i, (i + by) % size) for i in range(size)])


def ring_gather(up, low):
    left_up, right_low = shift(up, "y", 4, 1), shift(low, "y", 4, 3)
    left_low, right_up = shift(low, "y", 4, 1), shift(up, "y", 4, 3)
    far_up, far_low = shift(left_up, "y", 4, 1), shift(right_low, "y", 4, 3)
    return left_up, left_low, right_up, right_low, far_up, far_low


def halves(rows):
    return rows[: rows.shape[0] // 2], rows[rows.shape[0] // 2 :]


def after(value, *others):
    return lax.optimization_barrier((value, *others))[0]


def reduce_grad(keep, send):
    total = (keep + shift(send, "core", 2, 1)).astype(bf16).reshape(16, 32, FEAT)
    total = lax.all_to_all(total, ("x", "y"), 0, 0, tiled=True)
    total = total.reshape(4, 8, 16, FEAT).astype(f32).sum(0)
    across = lax.all_to_all(total, "z", 0, 0, tiled=True)
    return across.sum(0) * layer_share(LAYERS - 1)


def body(history, send_rows, batch_ids, block_cols, block_count, adjacency, weights, cotangent):
    me = lax.axis_index("y").astype(jnp.int32).reshape(1)
    core = lax.axis_index("core").astype(jnp.int32).reshape(1)
    by_step = lambda ids: ids.reshape(-1, ROWS // BLK, BLK).transpose(0, 2, 1)
    send_ids = by_step(send_rows)

    def exchange(rows):
        rows = rows.reshape(64, HALO // 64, FEAT)
        return lax.all_to_all(rows, TRAINER, 0, 0, tiled=True).reshape(HALO, FEAT)

    def exchange_chips(rows):
        rows = rows.reshape(32, 2 * H, FEAT)
        return lax.all_to_all(rows, ("z", "x"), 0, 0, tiled=True).reshape(HALO, FEAT)

    zero = history[0]
    sent = send_first(send_ids, zero)
    halo = exchange(sent)
    by_core = send_rows.reshape(32, 2, H)
    for_core = lambda at: lax.dynamic_index_in_dim(by_core, at, 1, False)
    by_chips = lambda ids: ids.reshape(-1, CHIPS * H // BLK, BLK).transpose(0, 2, 1)
    other_history = shift(after(history[1:], sent), "core", 2, 1)
    other_ids = shift(after(for_core(1 - core[0]), sent), "core", 2, 1)
    own_cot = after(cotangent, sent)
    others_cot = tuple(shift(own_cot, "y", 4, by) for by in (1, 3, 2))
    send_one, send_two = send_rest(core, by_chips(for_core(core[0])), by_chips(other_ids), history, other_history)
    start = start_rows(by_step(batch_ids), zero)
    halo_one = exchange_chips(after(send_one, start, *others_cot))

    support = layer(block_cols, block_count, halves(start), halo, start, adjacency)
    one = mix(0, me, support, ring_gather(*support), weights)
    halo_two = exchange_chips(after(send_two, *one))
    fresh = write_rows(0, batch_ids, history, one)
    support = layer(block_cols, block_count, one, halo_one, start, adjacency)
    two = mix(1, me, support, ring_gather(*support), weights)
    fresh = write_rows(1, batch_ids, history, two, fresh)
    support = layer(block_cols, block_count, after(tuple(two), fresh), halo_two, start, adjacency)
    others = ring_gather(*support)
    grad = reduce_grad(*grad_terms(core, me, support, cotangent, others_cot))
    final = mix_last(me, support, others, weights)
    return fresh, final, grad


def solution(mesh):
    fine = Mesh(mesh.devices.reshape(8, 4, 2, 4), ("z", "x", "core", "y"))
    return jax.shard_map(
        body,
        mesh=fine,
        in_specs=(
            P(None, TRAINER, "y"),
            P(TRAINER, None, None),
            P(TRAINER, None),
            P(TRAINER, None),
            P(TRAINER),
            P(TRAINER, None, None, None),
            P(None, None, "y"),
            P(TRAINER, "y"),
        ),
        out_specs=(P(None, TRAINER, "y"), P(TRAINER, "y"), P(TRAINER, "y")),
        check_vma=False,
    )
```

```python
import functools
import math

import jax
import jax.numpy as jnp
from jax import lax
from jax.experimental import pallas as pl
from jax.experimental.pallas import tpu as pltpu
from jax.sharding import Mesh
from jax.sharding import PartitionSpec as P

LAYERS = 3
BLK = 128
FEAT = 256
BATCH = 1024
HALF = 512
HALO = 3072
H = 48
CHIPS = 8
HIST = 2048
ROWS = 512
TALL = 1024
SLOTS = 12
RB = 8
HB = HALO // BLK
LATE = 10**11
TRAINER = ("z", "x", "core")

mixing = 0.1
strength = 0.5
bf16 = jnp.bfloat16
f32 = jnp.float32

VMEM = pl.BlockSpec(memory_space=pltpu.VMEM)
SMEM = pl.BlockSpec(memory_space=pltpu.SMEM)


def layer_share(layer_index):
    return math.log(strength / (layer_index + 1) + 1.0)


def call(kernel, name, flops, mib=12, **rest):
    return pl.pallas_call(
        kernel,
        name=name,
        compiler_params=pltpu.CompilerParams(vmem_limit_bytes=mib * 2**20),
        cost_estimate=pl.CostEstimate(flops=flops, bytes_accessed=4 << 20, transcendentals=0),
        **rest,
    )


def shape(*dims, dtype=bf16):
    return jax.ShapeDtypeStruct(dims, dtype)


def one_hot_of(ids):
    at = lax.broadcasted_iota(jnp.int32, (BLK, HIST), 1)
    parts = [(at == ids[:, b : b + 1]).astype(f32).astype(bf16) for b in range(ids.shape[1])]
    return jnp.concatenate(parts, 0)


def pick(chosen, rows):
    return jnp.dot(chosen, rows, preferred_element_type=f32).astype(bf16)


IDS = pl.BlockSpec((1, BLK, ROWS // BLK), lambda i: (i, 0, 0))


def send_first_kernel(ids_ref, rows_ref, out_ref):
    out_ref[...] = pick(one_hot_of(ids_ref[0]), rows_ref[...])


def send_first(ids, rows):
    return call(
        send_first_kernel,
        "send_first",
        2 * HALO * HIST * FEAT,
        mib=24,
        grid=(HALO // TALL,),
        in_specs=[pl.BlockSpec((1, BLK, TALL // BLK), lambda i: (i, 0, 0)), pl.BlockSpec((HIST, FEAT), lambda i: (0, 0))],
        out_specs=pl.BlockSpec((TALL, FEAT), lambda i: (i, 0)),
        out_shape=shape(HALO, FEAT),
    )(ids, rows)


def send_rest_kernel(core_ref, mine_ref, theirs_ref, own_one_ref, own_two_ref, other_ref, one_ref, two_ref):
    for core, ids_ref, one, two in (
        (core_ref[0], mine_ref, own_one_ref.at[0], own_two_ref.at[0]),
        (1 - core_ref[0], theirs_ref, other_ref.at[0], other_ref.at[1]),
    ):
        chosen = one_hot_of(ids_ref[0])
        one_ref[:, core] = pick(chosen, one[...]).reshape(CHIPS, H, FEAT)
        two_ref[:, core] = pick(chosen, two[...]).reshape(CHIPS, H, FEAT)


def send_rest(core, mine, theirs, history, other):
    ids = pl.BlockSpec((1, BLK, CHIPS * H // BLK), lambda i: (i, 0, 0))
    whole = lambda layer: pl.BlockSpec((1, HIST, FEAT), lambda i: (layer, 0, 0))
    rows = pl.BlockSpec((CHIPS, 2, H, FEAT), lambda i: (i, 0, 0, 0))
    return call(
        send_rest_kernel,
        "send_rest",
        4 * HALO * HIST * FEAT,
        mib=60,
        grid=(32 // CHIPS,),
        in_specs=[SMEM, ids, ids, whole(1), whole(2), pl.BlockSpec((2, HIST, FEAT), lambda i: (0, 0, 0))],
        out_specs=[rows, rows],
        out_shape=[shape(32, 2, H, FEAT)] * 2,
    )(core, mine, theirs, history, history, other)


def start_kernel(ids_ref, zero_ref, out_ref):
    out_ref[...] = pick(one_hot_of(ids_ref[0]), zero_ref[...])


def start_rows(ids, zero):
    return call(
        start_kernel,
        "start_rows",
        flops=2 * BATCH * HIST * FEAT,
        mib=60,
        grid=(BATCH // ROWS,),
        in_specs=[IDS, pl.BlockSpec((HIST, FEAT), lambda i: (0, 0))],
        out_specs=pl.BlockSpec((ROWS, FEAT), lambda i: (i, 0)),
        out_shape=shape(BATCH, FEAT),
    )(ids, zero)


def slab(w_ref, me, by):
    at = lax.rem(me + by, 4) * FEAT
    return w_ref[0, pl.ds(pl.multiple_of(at, FEAT), FEAT), :]


def mixed(share, me, w_ref, refs):
    own = refs[0][...]
    total = jnp.zeros(own.shape, f32)
    for ref, by in zip(refs, (0, 3, 1, 2)):
        total += jnp.dot(ref[...], slab(w_ref, me, by), preferred_element_type=f32)
    return (1.0 - share) * own.astype(f32) + share * total


def product(r, cols_ref, count_ref, adj_ref, x_ref):
    total = jnp.zeros((BLK, FEAT), f32)
    count = count_ref[r]
    for k in range(0, SLOTS, 2):
        left, right = [], []
        for slot in (k, k + 1):
            block = adj_ref[r, slot]
            left.append(jnp.where(slot < count, block, jnp.zeros_like(block)))
            right.append(x_ref[cols_ref[r, slot]])
        total += jnp.dot(jnp.concatenate(left, 1), jnp.concatenate(right, 0), preferred_element_type=f32)
    return total


def block(r):
    return pl.ds(r * BLK, BLK)


def put(up_ref, low_ref, r, value):
    ref = up_ref if r < RB // 2 else low_ref
    ref[block(r % (RB // 2)), :] = value


def supported(total, start_ref, r):
    return ((1.0 - mixing) * total + mixing * start_ref[block(r), :].astype(f32)).astype(bf16)


def layer_kernel(cols_ref, count_ref, up_ref, low_ref, halo_ref, start_ref, adj_ref, out_up_ref, out_low_ref, x_ref):
    x_ref[: RB // 2] = up_ref[...].reshape(RB // 2, BLK, FEAT)
    x_ref[RB // 2 : RB] = low_ref[...].reshape(RB // 2, BLK, FEAT)
    x_ref[RB:] = halo_ref[...].reshape(HB, BLK, FEAT)
    for r in range(RB):
        put(out_up_ref, out_low_ref, r, supported(product(r, cols_ref, count_ref, adj_ref, x_ref), start_ref, r))


def layer(cols, count, rows, halo, start, adjacency):
    return call(
        layer_kernel,
        "layer",
        2 * BATCH * SLOTS * BLK * FEAT,
        in_specs=[SMEM, SMEM] + [VMEM] * 5,
        out_specs=[VMEM, VMEM],
        out_shape=[shape(HALF, FEAT)] * 2,
        scratch_shapes=[pltpu.VMEM((RB + HB, BLK, FEAT), bf16)],
    )(cols, count, *rows, halo, start, adjacency)


def mix_kernel(share, me_ref, up_ref, low_ref, lu_ref, ll_ref, ru_ref, rl_ref, fu_ref, fl_ref, w_ref, out_up_ref, out_low_ref):
    me = me_ref[0]
    out_up_ref[...] = jnp.maximum(mixed(share, me, w_ref, (up_ref, lu_ref, ru_ref, fu_ref)), 0.0).astype(bf16)
    out_low_ref[...] = jnp.maximum(mixed(share, me, w_ref, (low_ref, ll_ref, rl_ref, fl_ref)), 0.0).astype(bf16)


def mix(index, me, rows, others, weights):
    half = pl.BlockSpec((HALF, FEAT), lambda i: (0, 0))
    return call(
        functools.partial(mix_kernel, layer_share(index)),
        "mix",
        2 * BATCH * 4 * FEAT * FEAT,
        grid=(1,),
        in_specs=[SMEM] + [half] * 8 + [pl.BlockSpec((1, 4 * FEAT, FEAT), lambda i: (index, 0, 0))],
        out_specs=[half, half],
        out_shape=[shape(HALF, FEAT)] * 2,
    )(me, *rows, *others, weights)


def mix_last_kernel(me_ref, up_ref, low_ref, lu_ref, ll_ref, ru_ref, rl_ref, fu_ref, fl_ref, w_ref, out_ref):
    me, share = me_ref[0], layer_share(2)
    out_ref[:HALF] = mixed(share, me, w_ref, (up_ref, lu_ref, ru_ref, fu_ref)).astype(bf16)
    out_ref[HALF:] = mixed(share, me, w_ref, (low_ref, ll_ref, rl_ref, fl_ref)).astype(bf16)


def mix_last(me, rows, others, weights):
    half = pl.BlockSpec((HALF, FEAT), lambda i: (0, 0))
    return call(
        mix_last_kernel,
        "mix_last",
        LATE,
        grid=(1,),
        in_specs=[SMEM] + [half] * 8 + [pl.BlockSpec((1, 4 * FEAT, FEAT), lambda i: (2, 0, 0))],
        out_specs=pl.BlockSpec((BATCH, FEAT), lambda i: (0, 0)),
        out_shape=shape(BATCH, FEAT),
    )(me, *rows, *others, weights)


def write_kernel(ids_ref, history_ref, *refs):
    base = pl.program_id(0) * ROWS
    at = lax.broadcasted_iota(jnp.int32, (ROWS, BATCH), 0) + base
    chosen = (at == ids_ref[...]).astype(f32)
    hit = jnp.max(chosen, axis=1, keepdims=True) > 0.0
    rows = jnp.concatenate([refs[0][...], refs[1][...]], 0)
    refs[-1][0] = jnp.where(hit, pick(chosen.astype(bf16), rows), history_ref[0])


def write_rows(layer, ids, history, rows, so_far=None):
    in_specs = [
        pl.BlockSpec((1, BATCH), lambda i: (0, 0)),
        pl.BlockSpec((1, ROWS, FEAT), lambda i: (layer + 1, i, 0)),
    ] + [pl.BlockSpec(part.shape, lambda i: (0, 0)) for part in rows]
    if so_far is not None:
        in_specs.append(pl.BlockSpec(memory_space=pl.ANY))
    return call(
        write_kernel,
        "write_rows",
        2 * BATCH * HIST * FEAT,
        grid=(HIST // ROWS,),
        in_specs=in_specs,
        out_specs=pl.BlockSpec((1, ROWS, FEAT), lambda i: (layer, i, 0)),
        out_shape=shape(2, HIST, FEAT),
        input_output_aliases={} if so_far is None else {len(in_specs) - 1: 0},
    )(ids, history, *rows, *(() if so_far is None else (so_far,)))


def grad_kernel(core_ref, me_ref, up_ref, low_ref, own_ref, left_ref, right_ref, far_ref, keep_ref, send_ref, acc_ref):
    support = jnp.concatenate([up_ref[...], low_ref[...]], 0)
    for by, ref in ((0, own_ref), (3, left_ref), (1, right_ref), (2, far_ref)):
        term = lax.dot_general(support, ref[...], (((0,), (0,)), ((), ())), preferred_element_type=f32)
        acc_ref[lax.rem(me_ref[0] + by, 4)] = term.reshape(8, 32, FEAT)
    mine = pl.multiple_of(core_ref[0] * 16, 16)
    theirs = pl.multiple_of(16 - core_ref[0] * 16, 16)
    for low in range(2):
        for x in range(4):
            group = low * 4 + x
            for y in range(4):
                keep_ref[x * 4 + y, low] = acc_ref[y, group, pl.ds(mine, 16), :]
                send_ref[x * 4 + y, low] = acc_ref[y, group, pl.ds(theirs, 16), :]


def grad_terms(core, me, support, own, parts):
    return call(
        grad_kernel,
        "grad_terms",
        2 * BATCH * FEAT * 4 * FEAT,
        in_specs=[SMEM, SMEM] + [VMEM] * 6,
        out_specs=[VMEM, VMEM],
        out_shape=[shape(16, 2, 16, FEAT, dtype=f32)] * 2,
        scratch_shapes=[pltpu.VMEM((4, 8, 32, FEAT), f32)],
    )(core, me, *support, own, *parts)


def shift(array, axis, size, by):
    return lax.ppermute(array, axis, [(i, (i + by) % size) for i in range(size)])


def ring_gather(up, low):
    left_up, right_low = shift(up, "y", 4, 1), shift(low, "y", 4, 3)
    left_low, right_up = shift(low, "y", 4, 1), shift(up, "y", 4, 3)
    far_up, far_low = shift(left_up, "y", 4, 1), shift(right_low, "y", 4, 3)
    return left_up, left_low, right_up, right_low, far_up, far_low


def halves(rows):
    return rows[: rows.shape[0] // 2], rows[rows.shape[0] // 2 :]


def after(value, *others):
    return lax.optimization_barrier((value, *others))[0]


def reduce_grad(keep, send):
    total = (keep + shift(send, "core", 2, 1)).astype(bf16).reshape(16, 32, FEAT)
    total = lax.all_to_all(total, ("x", "y"), 0, 0, tiled=True)
    total = total.reshape(4, 8, 16, FEAT).astype(f32).sum(0)
    across = lax.all_to_all(total, "z", 0, 0, tiled=True)
    return across.sum(0) * layer_share(LAYERS - 1)


def body(history, send_rows, batch_ids, block_cols, block_count, adjacency, weights, cotangent):
    me = lax.axis_index("y").astype(jnp.int32).reshape(1)
    core = lax.axis_index("core").astype(jnp.int32).reshape(1)
    by_step = lambda ids: ids.reshape(-1, ROWS // BLK, BLK).transpose(0, 2, 1)
    send_ids = send_rows.reshape(-1, TALL // BLK, BLK).transpose(0, 2, 1)

    def exchange(rows):
        rows = rows.reshape(64, HALO // 64, FEAT)
        return lax.all_to_all(rows, TRAINER, 0, 0, tiled=True).reshape(HALO, FEAT)

    def exchange_chips(rows):
        rows = rows.reshape(32, 2 * H, FEAT)
        return lax.all_to_all(rows, ("z", "x"), 0, 0, tiled=True).reshape(HALO, FEAT)

    zero = history[0]
    sent = send_first(send_ids, zero)
    halo = exchange(sent)
    by_core = send_rows.reshape(32, 2, H)
    for_core = lambda at: lax.dynamic_index_in_dim(by_core, at, 1, False)
    by_chips = lambda ids: ids.reshape(-1, CHIPS * H // BLK, BLK).transpose(0, 2, 1)
    other_history = shift(after(history[1:], sent), "core", 2, 1)
    other_ids = shift(after(for_core(1 - core[0]), sent), "core", 2, 1)
    own_cot = after(cotangent, sent)
    others_cot = tuple(shift(own_cot, "y", 4, by) for by in (1, 3, 2))
    send_one, send_two = send_rest(core, by_chips(for_core(core[0])), by_chips(other_ids), history, other_history)
    start = start_rows(by_step(batch_ids), zero)
    halo_one = exchange_chips(after(send_one, start, *others_cot))

    support = layer(block_cols, block_count, halves(start), halo, start, adjacency)
    one = mix(0, me, support, ring_gather(*support), weights)
    halo_two = exchange_chips(after(send_two, *one))
    fresh = write_rows(0, batch_ids, history, one)
    support = layer(block_cols, block_count, one, halo_one, start, adjacency)
    two = mix(1, me, support, ring_gather(*support), weights)
    fresh = write_rows(1, batch_ids, history, two, fresh)
    support = layer(block_cols, block_count, after(tuple(two), fresh), halo_two, start, adjacency)
    others = ring_gather(*support)
    grad = reduce_grad(*grad_terms(core, me, support, cotangent, others_cot))
    final = mix_last(me, support, others, weights)
    return fresh, final, grad


def solution(mesh):
    fine = Mesh(mesh.devices.reshape(8, 4, 2, 4), ("z", "x", "core", "y"))
    return jax.shard_map(
        body,
        mesh=fine,
        in_specs=(
            P(None, TRAINER, "y"),
            P(TRAINER, None, None),
            P(TRAINER, None),
            P(TRAINER, None),
            P(TRAINER),
            P(TRAINER, None, None, None),
            P(None, None, "y"),
            P(TRAINER, "y"),
        ),
        out_specs=(P(None, TRAINER, "y"), P(TRAINER, "y"), P(TRAINER, "y")),
        check_vma=False,
    )
```
